32 devices in a mesh: row: 4 (over x, core), col: 4 (over z), layer: 2 (over y).
Axes of the slice: x: 2, y: 2, z: 4, core: 2. Of those that a mesh axis runs over, the one named last changes fastest.
Arguments:
- p_vals: bfloat16 [2048, 12, 64, 64], P(('row', 'col', 'layer')), may hold values from -0.59765625 to 0.59765625
- block_cols: int32 [2048, 12], replicated, may hold values from -1 to 2047, as said below
Outputs:
- p_next: bfloat16 [2048, 12, 64, 64], P(('row', 'col', 'layer'))
The draws below stay inside these ranges and needn't reach their ends.
Inputs may be any that keep to these rules, and one draw needn't show every extreme that they name: `block_cols`: each block row i lists distinct block columns within 8 of i in its first slots, its own column i in slot 0; it lists 12//2 or more of them, or all that its band holds near the matrix's ends, and block row 1024 lists 12; the remaining slots hold -1.
All inputs are finite; a program needn't handle non-finite values.
Results may differ from the reference program's by a relative error of at most 0.0043.
Values may be sent and summed in bfloat16 or wider, within the bound.
A program may use at most 128 MiB of HBM per device.

```python
import jax
import jax.numpy as jnp
from jax import lax

BS = 64
NB = 2048
KMAX = 12
HALF = 8
GROUP_ROWS = 16
N_ROW = 4
N_COL = 4
N_LAYER = 2


def draw_block_cols(key, part):
    width = 2 * HALF + 1
    keys = jax.random.split(jax.random.fold_in(key, 11), NB)
    perms = jax.vmap(lambda one: jax.random.permutation(one, width))(keys).astype(jnp.int32)
    rows = jnp.arange(NB, dtype=jnp.int32)[:, None]
    offsets = perms - HALF
    candidates = rows + offsets
    inside = (candidates >= 0) & (candidates < NB)
    places = jnp.arange(width, dtype=jnp.int32)[None, :]
    score = jnp.where(offsets == 0, 0, jnp.where(inside, 1 + places, width + 1 + places))
    order = jnp.argsort(score, axis=1, stable=True)
    chosen = jnp.take_along_axis(candidates, order, axis=1)[:, :KMAX]
    inside_count = jnp.sum(inside.astype(jnp.int32), axis=1)
    counts = jax.random.randint(jax.random.fold_in(key, 12), (NB,), KMAX // 2, KMAX + 1)
    counts = jnp.where(jnp.arange(NB, dtype=jnp.int32) == NB // 2, KMAX, counts)
    counts = jnp.minimum(counts, inside_count)
    slots = jnp.arange(KMAX, dtype=jnp.int32)[None, :]
    return jnp.where(slots < counts[:, None], chosen, -1).astype(jnp.int32)


def levels(stream_key, dims, cuts, low, top_value):
    factor_of, own = 1.0, jax.random.fold_in(stream_key, 6)
    for position, shards_of in cuts:
        steps = jnp.exp(jax.random.uniform(jax.random.fold_in(own, position), (shards_of,), jnp.float32, low / len(cuts), top_value / len(cuts)))
        factor_of = factor_of * jnp.repeat(steps, dims[position] // shards_of).reshape([-1 if axis == position else 1 for axis in range(len(dims))])
    return factor_of


def centred(stream_key, extent, spread, reach, cuts=(), kind=jnp.bfloat16):
    values = jax.random.normal(stream_key, extent, jnp.float32) * spread
    if len(cuts) > 0:
        values = levels(stream_key, extent, cuts, -0.22, 0.18) * values
    return jnp.clip(values, min=-reach, max=reach).astype(kind)


def setup_inputs(seed: int = 0) -> dict:
    seeds = jax.random.split(jax.random.key(seed), 3)
    p_vals = centred(seeds[0], (NB, KMAX, BS, BS), 0.1, 0.59765625, ((0, 32),))
    block_cols = draw_block_cols(jax.random.fold_in(seeds[2], 71), 0)
    return dict(p_vals=p_vals, block_cols=block_cols)


def reorder(blocks):
    rest = blocks.shape[1:]
    shaped = blocks.reshape((N_ROW, N_COL, N_LAYER, N_COL, GROUP_ROWS) + rest)
    shaped = jnp.transpose(shaped, (0, 3, 2, 1, 4) + tuple(range(5, 5 + len(rest))))
    return shaped.reshape((NB,) + rest)


def select_blocks(row_cols, table, block_cols, offset):
    live_b = row_cols >= 0
    k_rows = jnp.clip(row_cols, 0, NB - 1).astype(jnp.int32)
    k_cols = block_cols[k_rows]
    match = (k_cols[None, :, :] == row_cols[:, None, None]) & (row_cols >= 0)[:, None, None] & live_b[None, :, None]
    found = jnp.any(match, axis=-1)
    where_c = jnp.argmax(match, axis=-1).astype(jnp.int32)
    local = jnp.clip(k_rows - offset, 0, table.shape[0] - 1).astype(jnp.int32)
    picked = table[local[None, :], where_c]
    return jnp.where(found[:, :, None, None], picked, jnp.zeros_like(picked))


def reference(p_vals, block_cols):
    band = reorder(p_vals)

    def one_row(i):
        row_cols = block_cols[i]
        chosen = select_blocks(row_cols, band, block_cols, 0).astype(jnp.float32)
        own = band[i].astype(jnp.float32)
        q_block = jnp.einsum("bxy,abyz->axz", own, chosen)
        q_half = q_block.astype(jnp.bfloat16).astype(jnp.float32)
        r_block = jnp.einsum("bxy,abyz->axz", q_half, chosen)
        return (3.0 * q_block - 2.0 * r_block).astype(jnp.bfloat16)

    result = lax.map(one_row, jnp.arange(NB, dtype=jnp.int32))
    return reorder(result)
```

```python
import functools

import jax
import jax.numpy as jnp
from jax import lax
from jax.experimental import pallas as pl
from jax.experimental.pallas import tpu as pltpu
from jax.sharding import PartitionSpec as P

HALF = 8
BAND = 2 * HALF + 1
PREFIXES, CAP_B = (36, 60, 84), 36


def with_halo(cells, sides, width):
    for axis, dim in sides:
        count = lax.axis_size(axis)
        ends = count - 1
        head = lax.slice_in_dim(cells, 0, width, axis=dim)
        tail = lax.slice_in_dim(cells, cells.shape[dim] - width, cells.shape[dim], axis=dim)
        cells = jnp.concatenate(
            [
                lax.ppermute(tail, axis, [(i, (i + 1) % count) for i in range(ends)]),
                cells,
                lax.ppermute(head, axis, [((i + 1) % count, i) for i in range(ends)]),
            ],
            axis=dim,
        )
    return cells


def group_frames(block_cols, group, slots, first_group, stride):
    kmax = block_cols.shape[1]
    padded = jnp.pad(block_cols, ((group, group), (0, 0)), constant_values=-1)
    rows, width = 3 * group, 3 * group + 2 * HALF
    firsts = (first_group + stride * jnp.arange(slots, dtype=jnp.int32)) * group
    cols = jnp.stack(
        [lax.dynamic_slice_in_dim(padded, firsts[j], rows, 0) for j in range(slots)]
    )
    base = firsts - group - HALF
    place = jnp.where(cols >= 0, cols - base[:, None, None], -1)
    match = place[..., None] == jnp.arange(width, dtype=jnp.int32)
    numbers = jnp.arange(kmax, dtype=jnp.int32)[:, None]
    slot = jnp.max(jnp.where(match, numbers, -1), axis=2)
    return place, slot


def shared(live, rows, cols):
    own = live[:, rows]
    return jnp.any(own[:, :, cols, None] & own[:, :, None, :], axis=1)


def ranks(needed, ahead):
    slots, rows, width = needed.shape
    pairs = needed.reshape(slots, rows * (width // 2), 2).astype(jnp.int32)

    def count(part):
        flat = part.reshape(-1, 2)
        size = flat.shape[0]
        before = (jnp.arange(size)[:, None] > jnp.arange(size)[None, :]).astype(jnp.bfloat16)
        seen = jnp.dot(before, flat.astype(jnp.bfloat16), preferred_element_type=jnp.float32)
        return seen.astype(jnp.int32).reshape(part.shape)

    return count(pairs[:ahead]), count(pairs[ahead:]), pairs


def pack_kernel(src_ref, p_ref, *outs):
    kmax = p_ref.shape[1]
    done = 0
    for out in outs:
        count = out.shape[0]

        def one(n, _, out=out, done=done):
            low = src_ref[2 * (done + n)]
            high = src_ref[2 * (done + n) + 1]
            left = p_ref[low // kmax, lax.rem(low, kmax)]
            right = p_ref[high // kmax, lax.rem(high, kmax)]
            out[n] = jnp.concatenate([left, right], axis=1)
            return 0

        lax.fori_loop(0, count, one, 0, unroll=6 if count % 6 == 0 else 2)
        done += count


def compute_kernel(start, own_tab, halo_tab, col_tab, mask_ref, p_ref, *refs):
    *bufs, out_ref, halo, dense, res = refs
    if start:
        bufs = bufs[:-1]
    here = pl.program_id(0)
    step = here + start
    group, kmax, bs = p_ref.shape[:3]
    wide = group + 2 * HALF
    tiles = wide // 2
    lane = lax.broadcasted_iota(jnp.int32, (bs, 2 * bs), 1)
    first_half = lane < bs
    total = sum(buf.shape[0] for buf in bufs)

    @pl.when(here == 0)
    def _():
        at = 0
        for buf in bufs:
            halo[at : at + buf.shape[0]] = buf[...]
            at += buf.shape[0]
        halo[at] = jnp.zeros((bs, 2 * bs), halo.dtype)
        dense[...] = jnp.zeros_like(dense)

    zero = jnp.zeros((bs, 2 * bs), dense.dtype)
    for f in range(wide):
        own = HALF <= f < HALF + group
        for t in range(max(0, (f - HALF) // 2), min(tiles - 1, (f + HALF) // 2) + 1):
            if own:
                at = (step * group + f - HALF) * wide + 2 * t
                low, high = own_tab[at], own_tab[at + 1]
                left = p_ref[f - HALF, jnp.maximum(low, 0)]
                right = p_ref[f - HALF, jnp.maximum(high, 0)]
                both = jnp.concatenate([left, right], axis=1)
                keep = (first_half & (low >= 0)) | (~first_half & (high >= 0))
                tile = jnp.where(keep, both, zero)
            else:
                h = f if f < HALF else f - group
                at = (step * 2 * HALF + h) * wide + 2 * t
                low, high = halo_tab[at], halo_tab[at + 1]
                low = jnp.where(low < 0, total, low)
                high = jnp.where(high < 0, total, high)
                tile = jnp.where(first_half, halo[low], halo[high])
            dense[f * bs : (f + 1) * bs, t * 2 * bs : (t + 1) * 2 * bs] = tile

    sub = 4
    span = (sub + 2 * HALF) * bs
    for s in range(group // sub):
        a0 = s * sub * bs
        rows = slice(HALF * bs + a0, HALF * bs + a0 + sub * bs)
        band = dense[a0 : a0 + span, a0 : a0 + span]
        q = jnp.dot(dense[rows, a0 : a0 + span], band, preferred_element_type=jnp.float32)
        mask = mask_ref[s * sub : (s + 1) * sub, :, a0 : a0 + span] > 0
        mask = jnp.broadcast_to(mask, (sub, bs, span)).reshape(sub * bs, span)
        qh = jnp.where(mask, q, 0.0).astype(jnp.bfloat16)
        r = jnp.dot(qh, band, preferred_element_type=jnp.float32)
        res[...] = (3.0 * q - 2.0 * r).astype(jnp.bfloat16)
        for i in range(sub):
            for a in range(kmax):
                row = s * sub + i
                col = col_tab[(step * group + row) * kmax + a]
                place = jnp.maximum(col - s * sub, 0)
                start = pl.multiple_of((place // 2) * 2 * bs, 2 * bs)
                pair = res[i * bs : (i + 1) * bs, pl.ds(start, 2 * bs)]
                odd = lax.rem(place, 2) == 1
                block = jnp.where(odd, pair[:, bs:], pair[:, :bs])
                out_ref[row, a] = jnp.where(col >= 0, block, jnp.zeros_like(block))


def multiply(first, count, group, tabs, mask, band, bufs, before=None):
    rows_here, kmax, bs = band.shape[:3]
    wide = group + 2 * HALF
    whole = [
        pl.BlockSpec(b.shape, lambda i, *_: (0, 0, 0), pipeline_mode=pl.Buffered(1)) for b in bufs
    ]
    step_rows = pl.BlockSpec((group, kmax, bs, bs), lambda i, *_: (i + first, 0, 0, 0))
    extra, alias = [], {}
    if before is not None:
        extra = [before]
        alias = {3 + 2 + len(bufs): 0}
    return pl.pallas_call(
        functools.partial(compute_kernel, first),
        grid_spec=pltpu.PrefetchScalarGridSpec(
            num_scalar_prefetch=3,
            grid=(count,),
            in_specs=[
                pl.BlockSpec((group, 1, wide * bs), lambda i, *_: (i + first, 0, 0)),
                step_rows,
                *whole,
                *[pl.BlockSpec(memory_space=pl.ANY) for _ in extra],
            ],
            out_specs=step_rows,
            scratch_shapes=[
                pltpu.VMEM((sum(b.shape[0] for b in bufs) + 1, bs, 2 * bs), band.dtype),
                pltpu.VMEM((wide * bs, wide * bs), band.dtype),
                pltpu.VMEM((4 * bs, (4 + 2 * HALF) * bs), band.dtype),
            ],
        ),
        out_shape=jax.ShapeDtypeStruct(band.shape, band.dtype),
        input_output_aliases=alias,
        compiler_params=pltpu.CompilerParams(vmem_limit_bytes=60 << 20),
        cost_estimate=pl.CostEstimate(flops=count * 10_000_000_000, bytes_accessed=count * 8_000_000, transcendentals=0),
    )(*tabs, mask, band, *bufs, *extra)


def pack(sources, blocks, counts):
    bs = blocks.shape[2]
    return pl.pallas_call(
        pack_kernel,
        grid_spec=pltpu.PrefetchScalarGridSpec(
            num_scalar_prefetch=1,
            grid=(1,),
            in_specs=[
                pl.BlockSpec(blocks.shape, lambda i, *_: (0, 0, 0, 0), pipeline_mode=pl.Buffered(1))
            ],
            out_specs=[pl.BlockSpec((n, bs, 2 * bs), lambda i, *_: (0, 0, 0)) for n in counts],
        ),
        out_shape=[jax.ShapeDtypeStruct((n, bs, 2 * bs), blocks.dtype) for n in counts],
        compiler_params=pltpu.CompilerParams(vmem_limit_bytes=56 << 20),
    )(sources, blocks)


def own_tables(place, slot, group, bs):
    slots = slot.shape[0]
    wide = group + 2 * HALF
    own = slice(group, 2 * group)
    own_tab = slot[:, own, group : group + wide]
    mask = jnp.broadcast_to((own_tab >= 0)[..., None], own_tab.shape + (bs,))
    mask = mask.astype(jnp.float32).reshape(slots * group, 1, wide * bs)
    col_tab = jnp.where(place[:, own] >= 0, place[:, own] - group, -1)
    return own_tab.reshape(-1), col_tab.reshape(-1), mask


def longest_lists(block_cols, group, n_row, n_col, n_layer):
    wide, ring, slots = group + 2 * HALF, n_layer * n_col, n_col
    count = block_cols.shape[0] // group
    padded = jnp.pad(block_cols, ((HALF, HALF), (0, 0)), constant_values=-1)
    kmax = block_cols.shape[1]
    lead = padded[: count * group].reshape(count, group, kmax)
    rest = padded[2 * HALF :].reshape(count, group, kmax)[:, group - 2 * HALF :]
    cols = jnp.concatenate([lead, rest], axis=1)
    base = jnp.arange(count, dtype=jnp.int32) * group - HALF
    place = jnp.where(cols >= 0, cols - base[:, None, None], -1)
    live = jnp.any(place[..., None] == jnp.arange(wide, dtype=jnp.int32), axis=2)
    own = live[:, HALF : HALF + group].astype(jnp.bfloat16)

    def needed(rows):
        both = jnp.einsum("gik,gic->gkc", own[:, :, rows], own, preferred_element_type=jnp.float32)
        hit = ((both > 0) & live[:, rows]).reshape(count, HALF, wide // 2, 2)
        return jnp.sum(hit.astype(jnp.int32), axis=(1, 2)).reshape(n_row, slots, ring, 2)

    place_in_ring = jnp.arange(ring)[None, None, :, None]
    up, dn = needed(slice(0, HALF)), needed(slice(HALF + group, wide))
    up = jnp.where(place_in_ring == 0, jnp.roll(up, -1, axis=1), up)
    dn = jnp.where(place_in_ring == ring - 1, dn, jnp.roll(dn, -1, axis=1))
    both = jnp.stack([up, dn])
    sums = [jnp.max(jnp.sum(both[:, :, :k], axis=2)) for k in range(1, slots)]
    return sums, jnp.max(both[:, :, slots - 1])


def halo_plan(p_vals, block_cols):
    n_row, n_col, n_layer = (lax.axis_size(a) for a in ("row", "col", "layer"))
    r, c, l = (lax.axis_index(a) for a in ("row", "col", "layer"))
    rows_here, kmax, bs = p_vals.shape[:3]
    slots = n_col
    group = rows_here // slots
    ring = n_layer * n_col
    idx = l * n_col + c
    wide = group + 2 * HALF
    axes = ("row", "col", "layer")
    everywhere = block_cols.shape[0] // group

    place, slot = group_frames(block_cols, group, slots, r * slots * ring + idx, ring)
    live = slot >= 0
    def cols_of(start, count):
        return slice(start + HALF, start + HALF + count)

    before, own, after = (slice(k * group, (k + 1) * group) for k in range(3))
    need_up = shared(live, own, cols_of(group - HALF, HALF)) & live[:, group - HALF : group]
    need_dn = shared(live, own, cols_of(2 * group, HALF)) & live[:, 2 * group : 2 * group + HALF]
    send_dn = shared(live, after, cols_of(2 * group - HALF, HALF)) & live[:, 2 * group - HALF : 2 * group]
    send_up = shared(live, before, cols_of(group, HALF)) & live[:, group : group + HALF]

    first, last = idx == 0, idx == ring - 1
    ahead = slots - 1
    in_up = jnp.where(first, jnp.roll(need_up, -1, axis=0), need_up)
    in_dn = jnp.where(last, need_dn, jnp.roll(need_dn, -1, axis=0))
    out_up = jnp.roll(send_up, -1, axis=0)
    (up_a, up_b, up_pairs), (dn_a, dn_b, dn_pairs) = ranks(in_up, ahead), ranks(in_dn, ahead)
    (so_a, so_b, so_pairs), (su_a, su_b, su_pairs) = ranks(send_dn, ahead), ranks(out_up, ahead)

    flat = lambda rr, ii: (rr * n_col + ii % n_col) * n_layer + ii // n_col
    ring_pairs = [
        (flat(rr, ii), flat(rr, (ii + 1) % ring)) for rr in range(n_row) for ii in range(ring)
    ]
    chain = [flat(n // ring, n % ring) for n in range(n_row * ring)]
    chain_pairs = list(zip(chain[:-1], chain[1:]))
    back = lambda pairs: [(b, a) for a, b in pairs]

    frame_slot = slot[:, :, :]
    numbers = jnp.arange(rows_here, dtype=jnp.int32).reshape(slots, group)
    source = jnp.maximum(frame_slot[:, own], 0) + numbers[:, :, None] * kmax
    src_dn = source[:, group - HALF :].reshape(slots, -1, 2)
    src_up = jnp.roll(source[:, :HALF], -1, axis=0).reshape(slots, -1, 2)

    def listed(rank, pairs, src, count):
        hit = (rank.reshape(-1, 1, 2) == jnp.arange(count, dtype=jnp.int32)[None, :, None]) & (
            pairs.reshape(-1, 1, 2) > 0
        )
        return jnp.sum(jnp.where(hit, src.reshape(-1, 1, 2), 0), axis=0)

    own_tab, col_tab, mask = own_tables(place, slot, group, bs)

    def exchange(ends_a, cap_b):
        cap_a = ends_a[-1]
        starts = (0,) + ends_a[:-1]
        pieces = []
        for rank_a, rank_b, pairs, src in (
            (su_a, su_b, su_pairs, src_up),
            (so_a, so_b, so_pairs, src_dn),
        ):
            pieces.append(listed(rank_b, pairs[ahead:], src[ahead:], cap_b))
            pieces.append(listed(rank_a, pairs[:ahead], src[:ahead], cap_a))
        sizes = (cap_b,) + tuple(b - a for a, b in zip(starts, ends_a))
        packed = pack(jnp.concatenate(pieces).reshape(-1), p_vals, sizes * 2)
        n = len(sizes)
        bufs, at = [], []
        total = 0
        for k in range(n):
            pairs = chain_pairs if k == 0 else ring_pairs
            bufs += [
                lax.ppermute(packed[n + k], axes, pairs),
                lax.ppermute(packed[k], axes, back(pairs)),
            ]
            at.append(total)
            total += 2 * sizes[k]

        def places(rank_a, rank_b, pairs, side):
            where_a = jnp.zeros_like(rank_a)
            for k in range(1, n):
                moved = rank_a - starts[k - 1] + at[k] + side * sizes[k]
                where_a = jnp.where(rank_a >= starts[k - 1], moved, where_a)
            where_b = rank_b + (at[0] + side * sizes[0])
            both = jnp.concatenate([where_a, where_b])
            return jnp.where(pairs > 0, both, -1).reshape(slots, HALF, -1)

        at_up = places(up_a, up_b, up_pairs, 0)
        at_up = jnp.where(first, jnp.roll(at_up, 1, axis=0), at_up)
        at_dn = places(dn_a, dn_b, dn_pairs, 1)
        at_dn = jnp.where(last, at_dn, jnp.roll(at_dn, 1, axis=0))
        halo_tab = jnp.concatenate([at_up, at_dn], axis=1)[..., group : group + wide]
        return bufs, (own_tab, halo_tab.reshape(-1), col_tab)

    def whole_path():
        half_band = (BAND + 1) // 2
        bufs, tabs = exchange((ahead * HALF * half_band,), HALF * half_band)
        return multiply(0, slots, group, tabs, mask, p_vals, bufs)

    if slots != len(PREFIXES) + 1:
        return whole_path()
    bufs, tabs = exchange(PREFIXES, CAP_B)

    def short_path():
        out = multiply(0, 1, group, tabs, mask, p_vals, bufs[:4])
        for k in range(1, slots - 1):
            count = 2 if k == slots - 2 else 1
            out = multiply(k, count, group, tabs, mask, p_vals, bufs[: 4 + 2 * k], out)
        return out

    sums, single = longest_lists(block_cols, group, n_row, n_col, n_layer)
    fits = single <= CAP_B
    for most, cap in zip(sums, PREFIXES):
        fits = fits & (most <= cap)
    return lax.cond(fits, short_path, whole_path)


def run_plan(p_vals, block_cols):
    rows, kmax, bs = p_vals.shape[:3]
    axes = ("row", "col", "layer")
    band = lax.all_to_all(p_vals, "col", split_axis=0, concat_axis=0, tiled=True)
    near = with_halo(band, ((axes, 0),), HALF)
    near = jnp.concatenate([near[:HALF], near[HALF + rows :]])
    place, slot = group_frames(block_cols, rows, 1, lax.axis_index(axes), 0)
    own_tab, col_tab, mask = own_tables(place, slot, rows, bs)
    wide = rows + 2 * HALF
    window = slice(rows, rows + wide)
    beside = jnp.concatenate([slot[0, rows - HALF : rows, window], slot[0, 2 * rows : 2 * rows + HALF, window]])
    listed = jnp.maximum(beside, 0) + jnp.arange(2 * HALF, dtype=jnp.int32)[:, None] * kmax
    count = HALF * wide
    bufs = pack(listed.reshape(-1), near, (count,))
    tile = jnp.arange(count, dtype=jnp.int32)[:, None]
    halo_tab = jnp.where(beside.reshape(-1, 2) >= 0, tile, -1).reshape(-1)
    out = multiply(0, 1, rows, (own_tab, halo_tab, col_tab), mask, band, bufs)
    return lax.all_to_all(out, "col", split_axis=0, concat_axis=0, tiled=True)


def per_device(p_vals, block_cols):
    group = p_vals.shape[0] // lax.axis_size("col")
    if group % 4 or group < 2 * HALF:
        return run_plan(p_vals, block_cols)
    return halo_plan(p_vals, block_cols)


def solution(mesh):
    placed = (P(("row", "col", "layer"), None, None, None), P())
    return jax.shard_map(
        per_device,
        mesh=mesh,
        in_specs=placed,
        out_specs=P(("row", "col", "layer"), None, None, None),
        check_vma=False,
    )
```

```python
import functools

import jax
import jax.numpy as jnp
from jax import lax
from jax.experimental import pallas as pl
from jax.experimental.pallas import tpu as pltpu
from jax.sharding import PartitionSpec as P

HALF = 8
BAND = 2 * HALF + 1
PREFIXES, CAP_B = (36, 60, 84), 36


def with_halo(cells, sides, width):
    for axis, dim in sides:
        count = lax.axis_size(axis)
        ends = count - 1
        head = lax.slice_in_dim(cells, 0, width, axis=dim)
        tail = lax.slice_in_dim(cells, cells.shape[dim] - width, cells.shape[dim], axis=dim)
        cells = jnp.concatenate(
            [
                lax.ppermute(tail, axis, [(i, (i + 1) % count) for i in range(ends)]),
                cells,
                lax.ppermute(head, axis, [((i + 1) % count, i) for i in range(ends)]),
            ],
            axis=dim,
        )
    return cells


def group_frames(block_cols, group, slots, first_group, stride):
    kmax = block_cols.shape[1]
    padded = jnp.pad(block_cols, ((group, group), (0, 0)), constant_values=-1)
    rows, width = 3 * group, 3 * group + 2 * HALF
    firsts = (first_group + stride * jnp.arange(slots, dtype=jnp.int32)) * group
    cols = jnp.stack(
        [lax.dynamic_slice_in_dim(padded, firsts[j], rows, 0) for j in range(slots)]
    )
    base = firsts - group - HALF
    place = jnp.where(cols >= 0, cols - base[:, None, None], -1)
    match = place[..., None] == jnp.arange(width, dtype=jnp.int32)
    numbers = jnp.arange(kmax, dtype=jnp.int32)[:, None]
    slot = jnp.max(jnp.where(match, numbers, -1), axis=2)
    return place, slot


def shared(live, rows, cols):
    own = live[:, rows]
    return jnp.any(own[:, :, cols, None] & own[:, :, None, :], axis=1)


def ranks(needed, ahead):
    slots, rows, width = needed.shape
    pairs = needed.reshape(slots, rows * (width // 2), 2).astype(jnp.int32)

    def count(part):
        flat = part.reshape(-1, 2)
        size = flat.shape[0]
        before = (jnp.arange(size)[:, None] > jnp.arange(size)[None, :]).astype(jnp.bfloat16)
        seen = jnp.dot(before, flat.astype(jnp.bfloat16), preferred_element_type=jnp.float32)
        return seen.astype(jnp.int32).reshape(part.shape)

    return count(pairs[:ahead]), count(pairs[ahead:]), pairs


def pack_kernel(src_ref, p_ref, *outs):
    kmax = p_ref.shape[1]
    done = 0
    for out in outs:
        count = out.shape[0]

        def one(n, _, out=out, done=done):
            low = src_ref[2 * (done + n)]
            high = src_ref[2 * (done + n) + 1]
            left = p_ref[low // kmax, lax.rem(low, kmax)]
            right = p_ref[high // kmax, lax.rem(high, kmax)]
            out[n] = jnp.concatenate([left, right], axis=1)
            return 0

        lax.fori_loop(0, count, one, 0, unroll=6 if count % 6 == 0 else 2)
        done += count


def compute_kernel(start, own_tab, halo_tab, col_tab, mask_ref, p_ref, *refs):
    *bufs, out_ref, halo, dense, res = refs
    if start:
        bufs = bufs[:-1]
    here = pl.program_id(0)
    step = here + start
    group, kmax, bs = p_ref.shape[:3]
    wide = group + 2 * HALF
    tiles = wide // 2
    lane = lax.broadcasted_iota(jnp.int32, (bs, 2 * bs), 1)
    first_half = lane < bs
    total = sum(buf.shape[0] for buf in bufs)

    @pl.when(here == 0)
    def _():
        at = 0
        for buf in bufs:
            halo[at : at + buf.shape[0]] = buf[...]
            at += buf.shape[0]
        halo[at] = jnp.zeros((bs, 2 * bs), halo.dtype)
        dense[...] = jnp.zeros_like(dense)

    zero = jnp.zeros((bs, 2 * bs), dense.dtype)
    for f in range(wide):
        own = HALF <= f < HALF + group
        for t in range(max(0, (f - HALF) // 2), min(tiles - 1, (f + HALF) // 2) + 1):
            if own:
                at = (step * group + f - HALF) * wide + 2 * t
                low, high = own_tab[at], own_tab[at + 1]
                left = p_ref[f - HALF, jnp.maximum(low, 0)]
                right = p_ref[f - HALF, jnp.maximum(high, 0)]
                both = jnp.concatenate([left, right], axis=1)
                keep = (first_half & (low >= 0)) | (~first_half & (high >= 0))
                tile = jnp.where(keep, both, zero)
            else:
                h = f if f < HALF else f - group
                at = (step * 2 * HALF + h) * wide + 2 * t
                low, high = halo_tab[at], halo_tab[at + 1]
                low = jnp.where(low < 0, total, jnp.minimum(low, total))
                high = jnp.where(high < 0, total, jnp.minimum(high, total))
                tile = jnp.where(first_half, halo[low], halo[high])
            dense[f * bs : (f + 1) * bs, t * 2 * bs : (t + 1) * 2 * bs] = tile

    sub = 4
    span = (sub + 2 * HALF) * bs
    for s in range(group // sub):
        a0 = s * sub * bs
        rows = slice(HALF * bs + a0, HALF * bs + a0 + sub * bs)
        band = dense[a0 : a0 + span, a0 : a0 + span]
        q = jnp.dot(dense[rows, a0 : a0 + span], band, preferred_element_type=jnp.float32)
        mask = mask_ref[s * sub : (s + 1) * sub, :, a0 : a0 + span] > 0
        mask = jnp.broadcast_to(mask, (sub, bs, span)).reshape(sub * bs, span)
        qh = jnp.where(mask, q, 0.0).astype(jnp.bfloat16)
        r = jnp.dot(qh, band, preferred_element_type=jnp.float32)
        res[...] = (3.0 * q - 2.0 * r).astype(jnp.bfloat16)
        for i in range(sub):
            for a in range(kmax):
                row = s * sub + i
                col = col_tab[(step * group + row) * kmax + a]
                place = jnp.maximum(col - s * sub, 0)
                start = pl.multiple_of((place // 2) * 2 * bs, 2 * bs)
                pair = res[i * bs : (i + 1) * bs, pl.ds(start, 2 * bs)]
                odd = lax.rem(place, 2) == 1
                block = jnp.where(odd, pair[:, bs:], pair[:, :bs])
                out_ref[row, a] = jnp.where(col >= 0, block, jnp.zeros_like(block))


def multiply(first, count, group, tabs, mask, band, bufs, before=None):
    rows_here, kmax, bs = band.shape[:3]
    wide = group + 2 * HALF
    whole = [
        pl.BlockSpec(b.shape, lambda i, *_: (0, 0, 0), pipeline_mode=pl.Buffered(1)) for b in bufs
    ]
    step_rows = pl.BlockSpec((group, kmax, bs, bs), lambda i, *_: (i + first, 0, 0, 0))
    extra, alias = [], {}
    if before is not None:
        extra = [before]
        alias = {3 + 2 + len(bufs): 0}
    return pl.pallas_call(
        functools.partial(compute_kernel, first),
        grid_spec=pltpu.PrefetchScalarGridSpec(
            num_scalar_prefetch=3,
            grid=(count,),
            in_specs=[
                pl.BlockSpec((group, 1, wide * bs), lambda i, *_: (i + first, 0, 0)),
                step_rows,
                *whole,
                *[pl.BlockSpec(memory_space=pl.ANY) for _ in extra],
            ],
            out_specs=step_rows,
            scratch_shapes=[
                pltpu.VMEM((sum(b.shape[0] for b in bufs) + 1, bs, 2 * bs), band.dtype),
                pltpu.VMEM((wide * bs, wide * bs), band.dtype),
                pltpu.VMEM((4 * bs, (4 + 2 * HALF) * bs), band.dtype),
            ],
        ),
        out_shape=jax.ShapeDtypeStruct(band.shape, band.dtype),
        input_output_aliases=alias,
        compiler_params=pltpu.CompilerParams(vmem_limit_bytes=60 << 20),
        cost_estimate=pl.CostEstimate(flops=count * 10_000_000_000, bytes_accessed=count * 8_000_000, transcendentals=0),
    )(*tabs, mask, band, *bufs, *extra)


def pack(sources, blocks, counts):
    bs = blocks.shape[2]
    return pl.pallas_call(
        pack_kernel,
        grid_spec=pltpu.PrefetchScalarGridSpec(
            num_scalar_prefetch=1,
            grid=(1,),
            in_specs=[
                pl.BlockSpec(blocks.shape, lambda i, *_: (0, 0, 0, 0), pipeline_mode=pl.Buffered(1))
            ],
            out_specs=[pl.BlockSpec((n, bs, 2 * bs), lambda i, *_: (0, 0, 0)) for n in counts],
        ),
        out_shape=[jax.ShapeDtypeStruct((n, bs, 2 * bs), blocks.dtype) for n in counts],
        compiler_params=pltpu.CompilerParams(vmem_limit_bytes=56 << 20),
    )(sources, blocks)


def own_tables(place, slot, group, bs):
    slots = slot.shape[0]
    wide = group + 2 * HALF
    own = slice(group, 2 * group)
    own_tab = slot[:, own, group : group + wide]
    mask = jnp.broadcast_to((own_tab >= 0)[..., None], own_tab.shape + (bs,))
    mask = mask.astype(jnp.float32).reshape(slots * group, 1, wide * bs)
    col_tab = jnp.where(place[:, own] >= 0, place[:, own] - group, -1)
    return own_tab.reshape(-1), col_tab.reshape(-1), mask


def longest_lists(block_cols, group, n_row, n_col, n_layer):
    wide, ring, slots = group + 2 * HALF, n_layer * n_col, n_col
    count = block_cols.shape[0] // group
    padded = jnp.pad(block_cols, ((HALF, HALF), (0, 0)), constant_values=-1)
    kmax = block_cols.shape[1]
    lead = padded[: count * group].reshape(count, group, kmax)
    rest = padded[2 * HALF :].reshape(count, group, kmax)[:, group - 2 * HALF :]
    cols = jnp.concatenate([lead, rest], axis=1)
    base = jnp.arange(count, dtype=jnp.int32) * group - HALF
    place = jnp.where(cols >= 0, cols - base[:, None, None], -1)
    live = jnp.any(place[..., None] == jnp.arange(wide, dtype=jnp.int32), axis=2)
    own = live[:, HALF : HALF + group].astype(jnp.bfloat16)

    def needed(rows):
        both = jnp.einsum("gik,gic->gkc", own[:, :, rows], own, preferred_element_type=jnp.float32)
        hit = ((both > 0) & live[:, rows]).reshape(count, HALF, wide // 2, 2)
        return jnp.sum(hit.astype(jnp.int32), axis=(1, 2)).reshape(n_row, slots, ring, 2)

    place_in_ring = jnp.arange(ring)[None, None, :, None]
    up, dn = needed(slice(0, HALF)), needed(slice(HALF + group, wide))
    up = jnp.where(place_in_ring == 0, jnp.roll(up, -1, axis=1), up)
    dn = jnp.where(place_in_ring == ring - 1, dn, jnp.roll(dn, -1, axis=1))
    both = jnp.stack([up, dn])
    sums = [jnp.max(jnp.sum(both[:, :, :k], axis=2)) for k in range(1, slots)]
    return sums, jnp.max(both[:, :, slots - 1])


def halo_plan(p_vals, block_cols):
    n_row, n_col, n_layer = (lax.axis_size(a) for a in ("row", "col", "layer"))
    r, c, l = (lax.axis_index(a) for a in ("row", "col", "layer"))
    rows_here, kmax, bs = p_vals.shape[:3]
    slots = n_col
    group = rows_here // slots
    ring = n_layer * n_col
    idx = l * n_col + c
    wide = group + 2 * HALF
    axes = ("row", "col", "layer")
    everywhere = block_cols.shape[0] // group

    place, slot = group_frames(block_cols, group, slots, r * slots * ring + idx, ring)
    live = slot >= 0
    def cols_of(start, count):
        return slice(start + HALF, start + HALF + count)

    before, own, after = (slice(k * group, (k + 1) * group) for k in range(3))
    need_up = shared(live, own, cols_of(group - HALF, HALF)) & live[:, group - HALF : group]
    need_dn = shared(live, own, cols_of(2 * group, HALF)) & live[:, 2 * group : 2 * group + HALF]
    send_dn = shared(live, after, cols_of(2 * group - HALF, HALF)) & live[:, 2 * group - HALF : 2 * group]
    send_up = shared(live, before, cols_of(group, HALF)) & live[:, group : group + HALF]

    first, last = idx == 0, idx == ring - 1
    ahead = slots - 1
    in_up = jnp.where(first, jnp.roll(need_up, -1, axis=0), need_up)
    in_dn = jnp.where(last, need_dn, jnp.roll(need_dn, -1, axis=0))
    out_up = jnp.roll(send_up, -1, axis=0)
    (up_a, up_b, up_pairs), (dn_a, dn_b, dn_pairs) = ranks(in_up, ahead), ranks(in_dn, ahead)
    (so_a, so_b, so_pairs), (su_a, su_b, su_pairs) = ranks(send_dn, ahead), ranks(out_up, ahead)

    flat = lambda rr, ii: (rr * n_col + ii % n_col) * n_layer + ii // n_col
    ring_pairs = [
        (flat(rr, ii), flat(rr, (ii + 1) % ring)) for rr in range(n_row) for ii in range(ring)
    ]
    chain = [flat(n // ring, n % ring) for n in range(n_row * ring)]
    chain_pairs = list(zip(chain[:-1], chain[1:]))
    back = lambda pairs: [(b, a) for a, b in pairs]

    frame_slot = slot[:, :, :]
    numbers = jnp.arange(rows_here, dtype=jnp.int32).reshape(slots, group)
    source = jnp.maximum(frame_slot[:, own], 0) + numbers[:, :, None] * kmax
    src_dn = source[:, group - HALF :].reshape(slots, -1, 2)
    src_up = jnp.roll(source[:, :HALF], -1, axis=0).reshape(slots, -1, 2)

    def listed(rank, pairs, src, count):
        hit = (rank.reshape(-1, 1, 2) == jnp.arange(count, dtype=jnp.int32)[None, :, None]) & (
            pairs.reshape(-1, 1, 2) > 0
        )
        return jnp.sum(jnp.where(hit, src.reshape(-1, 1, 2), 0), axis=0)

    own_tab, col_tab, mask = own_tables(place, slot, group, bs)

    def exchange(ends_a, cap_b):
        cap_a = ends_a[-1]
        starts = (0,) + ends_a[:-1]
        pieces = []
        for rank_a, rank_b, pairs, src in (
            (su_a, su_b, su_pairs, src_up),
            (so_a, so_b, so_pairs, src_dn),
        ):
            pieces.append(listed(rank_b, pairs[ahead:], src[ahead:], cap_b))
            pieces.append(listed(rank_a, pairs[:ahead], src[:ahead], cap_a))
        sizes = (cap_b,) + tuple(b - a for a, b in zip(starts, ends_a))
        packed = pack(jnp.concatenate(pieces).reshape(-1), p_vals, sizes * 2)
        n = len(sizes)
        bufs, at = [], []
        total = 0
        for k in range(n):
            pairs = chain_pairs if k == 0 else ring_pairs
            bufs += [
                lax.ppermute(packed[n + k], axes, pairs),
                lax.ppermute(packed[k], axes, back(pairs)),
            ]
            at.append(total)
            total += 2 * sizes[k]

        def places(rank_a, rank_b, pairs, side):
            where_a = jnp.zeros_like(rank_a)
            for k in range(1, n):
                moved = rank_a - starts[k - 1] + at[k] + side * sizes[k]
                where_a = jnp.where(rank_a >= starts[k - 1], moved, where_a)
            where_b = rank_b + (at[0] + side * sizes[0])
            both = jnp.concatenate([where_a, where_b])
            return jnp.where(pairs > 0, both, -1).reshape(slots, HALF, -1)

        at_up = places(up_a, up_b, up_pairs, 0)
        at_up = jnp.where(first, jnp.roll(at_up, 1, axis=0), at_up)
        at_dn = places(dn_a, dn_b, dn_pairs, 1)
        at_dn = jnp.where(last, at_dn, jnp.roll(at_dn, 1, axis=0))
        halo_tab = jnp.concatenate([at_up, at_dn], axis=1)[..., group : group + wide]
        return bufs, (own_tab, halo_tab.reshape(-1), col_tab)

    def whole_path():
        half_band = (BAND + 1) // 2
        bufs, tabs = exchange((ahead * HALF * half_band,), HALF * half_band)
        return multiply(0, slots, group, tabs, mask, p_vals, bufs)

    if slots != len(PREFIXES) + 1:
        return whole_path()
    bufs, tabs = exchange(PREFIXES, CAP_B)

    out = multiply(0, 1, group, tabs, mask, p_vals, bufs[:4])
    for k in range(1, slots - 2):
        out = multiply(k, 1, group, tabs, mask, p_vals, bufs[: 4 + 2 * k], out)

    def short_path():
        return multiply(slots - 2, 2, group, tabs, mask, p_vals, bufs, out)

    sums, single = longest_lists(block_cols, group, n_row, n_col, n_layer)
    fits = single <= CAP_B
    for most, cap in zip(sums, PREFIXES):
        fits = fits & (most <= cap)
    return lax.cond(fits, short_path, whole_path)


def run_plan(p_vals, block_cols):
    rows, kmax, bs = p_vals.shape[:3]
    axes = ("row", "col", "layer")
    band = lax.all_to_all(p_vals, "col", split_axis=0, concat_axis=0, tiled=True)
    near = with_halo(band, ((axes, 0),), HALF)
    near = jnp.concatenate([near[:HALF], near[HALF + rows :]])
    place, slot = group_frames(block_cols, rows, 1, lax.axis_index(axes), 0)
    own_tab, col_tab, mask = own_tables(place, slot, rows, bs)
    wide = rows + 2 * HALF
    window = slice(rows, rows + wide)
    beside = jnp.concatenate([slot[0, rows - HALF : rows, window], slot[0, 2 * rows : 2 * rows + HALF, window]])
    listed = jnp.maximum(beside, 0) + jnp.arange(2 * HALF, dtype=jnp.int32)[:, None] * kmax
    count = HALF * wide
    bufs = pack(listed.reshape(-1), near, (count,))
    tile = jnp.arange(count, dtype=jnp.int32)[:, None]
    halo_tab = jnp.where(beside.reshape(-1, 2) >= 0, tile, -1).reshape(-1)
    out = multiply(0, 1, rows, (own_tab, halo_tab, col_tab), mask, band, bufs)
    return lax.all_to_all(out, "col", split_axis=0, concat_axis=0, tiled=True)


def per_device(p_vals, block_cols):
    group = p_vals.shape[0] // lax.axis_size("col")
    if group % 4 or group < 2 * HALF:
        return run_plan(p_vals, block_cols)
    return halo_plan(p_vals, block_cols)


def solution(mesh):
    placed = (P(("row", "col", "layer"), None, None, None), P())
    return jax.shard_map(
        per_device,
        mesh=mesh,
        in_specs=placed,
        out_specs=P(("row", "col", "layer"), None, None, None),
        check_vma=False,
    )
```
